512 devices in a mesh: rep: 64 (over x, z_lo, y), fsdp: 8 (over z_hi, core).
Axes of the slice: x: 4, y: 8, z: 8 (z_hi: 4, z_lo: 2; z = z_hi * 2 + z_lo), core: 2. Of those that a mesh axis runs over, the one named last changes fastest.
Arguments:
- weights: bfloat16 [64, 2048, 2048], P('rep', None, 'fsdp'), may hold values from -0.125 to 0.125
- head_out: bfloat16 [64, 1024, 2048], P('rep', 'fsdp'), may hold values from -6 to 6
- token_ids: int32 [64, 1024], P('rep', 'fsdp'), may hold values from 0 to 31999, as said below
- embed_table: bfloat16 [32000, 2048], P('rep', 'fsdp'), may hold values from -6 to 6
- norm_gain: float32 [2048], replicated, may hold values from 0.1 to 1.9
- cotangent: bfloat16 [64, 1024, 2048], P('rep', 'fsdp'), may hold values from -6 to 6
- mix_step: int32 [1], replicated, may hold values from 0 to 999
Outputs:
- new_weights: bfloat16 [64, 2048, 2048], P('rep', None, 'fsdp')
The draws below stay inside these ranges and needn't reach their ends.
Inputs may be any that keep to these rules, and one draw needn't show every extreme that they name: `token_ids`: in each replica's 1024 tokens at most 32 ids lie in any one block of 500 ids that starts at a multiple of 500, and in each replica some block holds exactly 32 of them.
All inputs are finite; a program needn't handle non-finite values.
Results may differ from the reference program's by a relative error of at most 0.0039.
Values may be sent and summed in bfloat16 or wider, within the bound.
A program may use at most 64 MiB of HBM per device.

```python
import jax
import jax.numpy as jnp
from jax import lax

D = 2048
VOC_DEV = 500
MIXBITS = 4
HV = 2048
REPLICAS = 64
RT = 1024
VOCAB = 32000
CAP = 32
N_REP = 64


def replica_draw(replica_key):
    key_owner, key_noise, key_order, key_offset = jax.random.split(replica_key, 4)
    total_slots = N_REP * CAP
    full_owner = jax.random.randint(key_owner, (), 0, N_REP)
    slot_index = jnp.arange(total_slots, dtype=jnp.int32)
    noise_bits = jax.random.randint(key_noise, (total_slots,), 0, 1 << 16)
    scores = noise_bits * total_slots + slot_index
    scores = jnp.where(slot_index // CAP == full_owner, slot_index - total_slots, scores)
    ordering = jnp.argsort(scores, stable=True)[:RT]
    owners = (ordering // CAP).astype(jnp.int32)
    row_order = jax.random.permutation(key_order, RT)
    owners = owners[row_order]
    offsets = jax.random.randint(key_offset, (RT,), 0, VOC_DEV)
    return (owners * VOC_DEV + offsets).astype(jnp.int32)


def draw_token_ids(key, part):
    key = jax.random.fold_in(key, 11)
    replica_keys = jax.random.split(key, REPLICAS)
    return jax.vmap(replica_draw)(replica_keys)


def steps_of(rng, dims, cuts, smallest, high):
    def one(axis_at, shards_of):
        steps = jax.random.uniform(jax.random.fold_in(jax.random.fold_in(rng, 6), axis_at), (shards_of,), jnp.float32, smallest / len(cuts), high / len(cuts))
        return jnp.repeat(jnp.exp(steps), dims[axis_at] // shards_of).reshape((-1,) + (1,) * (len(dims) - axis_at - 1))

    factor_of = one(*cuts[0])
    for cut in cuts[1:]:
        factor_of = factor_of * one(*cut)
    return factor_of


def bell_draw(own_key, dims, spread, bound, cuts=(), held_as=jnp.bfloat16):
    array = jax.random.normal(own_key, dims, jnp.float32) * spread
    if len(cuts) > 0:
        array = steps_of(own_key, dims, cuts, -0.22, 0.18) * array
    return jnp.clip(array, min=-bound, max=bound).astype(held_as)


def setup_inputs(seed: int = 0) -> dict:
    key_list = jax.random.split(jax.random.key(seed), 8)
    weights = bell_draw(key_list[0], (REPLICAS, HV, D), HV ** -0.5, 0.125, ((0, 64), (2, 8)))
    head_out = bell_draw(key_list[1], (REPLICAS, RT, HV), 1.0, 6.0, ((0, 64), (1, 8)))
    token_ids = draw_token_ids(jax.random.fold_in(key_list[7], 71), 0)
    embed_table = bell_draw(key_list[3], (VOCAB, D), 1.0, 6.0, ((0, 64), (1, 8)))
    norm_gain = jnp.clip(1.0 + 0.18 * jax.random.normal(key_list[4], (D,), jnp.float32), 0.1, 1.9)
    cotangent = bell_draw(key_list[5], (REPLICAS, RT, D), 1.0, 6.0, ((0, 64), (1, 8)))
    mix_step = jax.random.randint(key_list[6], (1,), 0, 1000).astype(jnp.int32)
    return {"weights": weights, "head_out": head_out, "token_ids": token_ids, "embed_table": embed_table, "norm_gain": norm_gain, "cotangent": cotangent, "mix_step": mix_step}


EPS = 1e-05
RATE = 0.5

def reference(weights, head_out, token_ids, embed_table, norm_gain, cotangent, mix_step):
    mix_level = (mix_step[0] % MIXBITS).astype(jnp.int32)
    stride = jnp.left_shift(jnp.int32(1), mix_level)

    def replica(index):
        partner = jnp.bitwise_xor(index, stride).astype(jnp.int32)
        own_shard = lax.dynamic_index_in_dim(weights, index, 0, keepdims=False).astype(jnp.float32)
        other_shard = lax.dynamic_index_in_dim(weights, partner, 0, keepdims=False).astype(jnp.float32)
        mixed = (own_shard + other_shard) * 0.5
        mixed_weights = mixed.astype(jnp.bfloat16)
        head_rows = lax.dynamic_index_in_dim(head_out, index, 0, keepdims=False)
        id_rows = lax.dynamic_index_in_dim(token_ids, index, 0, keepdims=False)
        cot_rows = lax.dynamic_index_in_dim(cotangent, index, 0, keepdims=False)
        embedded = jnp.take(embed_table, id_rows, axis=0)
        stream = embedded.astype(jnp.float32) + jnp.dot(head_rows, mixed_weights, preferred_element_type=jnp.float32)
        inverse = 1.0 / jnp.sqrt(lax.optimization_barrier(jnp.mean(stream * stream, axis=-1, keepdims=True)) + EPS)
        weighted = norm_gain * cot_rows.astype(jnp.float32)
        drift = lax.optimization_barrier(jnp.mean(weighted * stream, axis=-1, keepdims=True))
        stream_grad = (weighted * inverse - stream * drift * inverse * inverse * inverse).astype(jnp.bfloat16)
        weight_grad = lax.dot_general(head_rows, stream_grad, (((0,), (0,)), ((), ())), preferred_element_type=jnp.float32) / RT
        return (mixed - RATE * weight_grad).astype(jnp.bfloat16)
    return lax.map(replica, jnp.arange(REPLICAS, dtype=jnp.int32))
```

```python
import functools

import jax
import jax.numpy as jnp
from jax import lax
from jax.experimental import pallas as pl
from jax.experimental.pallas import tpu as pltpu
from jax.sharding import PartitionSpec as P

MIXBITS = 4
EPS = 1e-05
RATE = 0.5
CAP = 32
MESH = pl.DeviceIdType.MESH
F32 = jnp.float32
BF16 = jnp.bfloat16
W_CHUNKS = 4

NT = (((1,), (1,)), ((), ()))
NN = (((1,), (0,)), ((), ()))


def dot(a, b, dims):
    return lax.dot_general(a, b, dims, preferred_element_type=F32)


def kernel(
    level, n_rep, n_fsdp,
    ids_ref, w_ref, h_ref, c_ref, tab_ref, gain_ref, out_ref,
    ids_all, w_own, w_other, heads, heads_t, cot, weighted_t, table, req_out, req_in, picked, fetched, mixed_t,
    stream_t, grad_t, stat_out, stat_in, position_row, gain_col,
    ids_send, ids_recv, w_send, w_recv, h_send, h_recv, c_send, c_recv, req_send, req_recv, row_send, row_recv,
    stat_send, stat_recv, local_sem,
):
    tokens, heads_width = h_ref.shape
    width = w_ref.shape[1]
    rows = w_ref.shape[0]
    features = width * n_fsdp
    all_tokens = tokens * n_fsdp
    vocab = tab_ref.shape[0]
    half = tokens // 2
    chunk = rows // W_CHUNKS
    rep = lax.axis_index("rep")
    me = lax.axis_index("fsdp")
    ring = n_fsdp // 2
    place, core = me // 2, me % 2
    up = (place + 1) % ring * 2 + core
    down = (place + ring - 1) % ring * 2 + core
    across = (place + 2) % ring * 2 + core
    sibling = place * 2 + 1 - core
    stride = 1 << level
    partner = rep + stride * (1 - 2 * (rep // stride % 2))

    def remote(src, dst, send, recv, r, f):
        return pltpu.make_async_remote_copy(
            src_ref=src, dst_ref=dst, send_sem=send, recv_sem=recv, device_id=(r, f), device_id_type=MESH
        )

    own_rows = pl.ds(pl.multiple_of(me * tokens, tokens), tokens)
    local = [
        pltpu.make_async_copy(w_ref, w_own, local_sem.at[0]),
        pltpu.make_async_copy(h_ref, heads.at[own_rows], local_sem.at[1]),
        pltpu.make_async_copy(
            c_ref.at[:, pl.ds(pl.multiple_of(me * width, width), width)], cot.at[me], local_sem.at[2]
        ),
    ]
    for copy in local:
        copy.start()

    barrier = pltpu.get_barrier_semaphore()

    @pl.loop(1, n_fsdp)
    def _(step):
        pl.semaphore_signal(barrier, inc=1, device_id=(rep, (me + step) % n_fsdp), device_id_type=MESH)

    @pl.loop(1, n_rep)
    def _(step):
        pl.semaphore_signal(barrier, inc=1, device_id=((rep + step) % n_rep, me), device_id_type=MESH)

    ids_all[me] = ids_ref[...]
    table[...] = jnp.zeros_like(table)
    table[:vocab] = tab_ref[...]
    gain = gain_ref[:, pl.ds(pl.multiple_of(me * width, width), width)]
    gain_col[...] = jnp.broadcast_to(gain, (128, width)).T

    pl.semaphore_wait(barrier, n_fsdp - 1 + n_rep - 1)

    def ids_copy(step):
        peer = (me + step) % n_fsdp
        return remote(ids_all.at[me], ids_all.at[me], ids_send.at[step], ids_recv.at[me], rep, peer)

    @pl.loop(1, n_fsdp)
    def _(step):
        ids_copy(step).start()

    def w_copy(k):
        part = pl.ds(k * chunk, chunk)
        return remote(w_ref.at[part], w_other.at[part], w_send.at[k], w_recv.at[k], partner, me)

    for k in range(W_CHUNKS):
        w_copy(k).start()

    def part_rows(owner, which):
        return pl.ds(pl.multiple_of(owner * tokens + which * half, half), half)

    def h_copy(index, owner, which, target, own=False):
        src = h_ref.at[pl.ds(which * half, half)] if own else heads.at[part_rows(owner, which)]
        return remote(
            src, heads.at[part_rows(owner, which)], h_send.at[index], h_recv.at[owner, which], rep, target
        )

    def h_wait(owner, which):
        h_copy(0, owner, which, sibling).wait_recv()

    own_sends = [
        h_copy(0, me, 0, up, True),
        h_copy(1, me, 1, down, True),
        h_copy(2, me, 1, up, True),
        h_copy(3, me, 0, down, True),
        h_copy(4, me, 0, sibling, True),
        h_copy(5, me, 1, sibling, True),
    ]
    for copy in own_sends:
        copy.start()

    def c_copy(step):
        peer = (me + step) % n_fsdp
        return remote(
            c_ref.at[:, pl.ds(pl.multiple_of(peer * width, width), width)],
            cot.at[me], c_send.at[step], c_recv.at[me], rep, peer,
        )

    @pl.loop(1, n_fsdp)
    def _(step):
        c_copy(step).start()

    @pl.loop(1, n_fsdp)
    def _(step):
        sender = (me + step) % n_fsdp
        remote(ids_all.at[me], ids_all.at[sender], ids_send.at[step], ids_recv.at[sender], rep, sender).wait_recv()

    ids_row = jnp.concatenate([ids_all[j] for j in range(n_fsdp)], axis=1)
    owner_row = ids_row // vocab
    local_row = ids_row - owner_row * vocab + 1
    block_iota = lax.broadcasted_iota(jnp.int32, (n_rep, all_tokens), 0)
    owned = block_iota == owner_row
    owned_b = jnp.where(owned, 1.0, 0.0).astype(BF16)
    earlier = (
        lax.broadcasted_iota(jnp.int32, (all_tokens, all_tokens), 0)
        < lax.broadcasted_iota(jnp.int32, (all_tokens, all_tokens), 1)
    )
    before = dot(owned_b, jnp.where(earlier, 1.0, 0.0).astype(BF16), NN)
    rank = jnp.sum(jnp.where(owned, before, 0.0), axis=0, keepdims=True).astype(jnp.int32)
    position_row[...] = owner_row * CAP + rank
    per_tile = 128 // CAP
    lane = rank + rep % per_tile * CAP
    here = lax.broadcasted_iota(jnp.int32, (128, all_tokens), 0) == lane
    high = jnp.where(here, (local_row // 2).astype(F32), 0.0).astype(BF16)
    low = jnp.where(here, (local_row % 2).astype(F32), 0.0).astype(BF16)
    requests = dot(owned_b, high, NT) * 2.0 + dot(owned_b, low, NT)
    for v in range(n_rep):
        req_out[v] = requests[v : v + 1]
    req_in[rep] = req_out[rep]

    def req_copy(step):
        peer = (rep + step) % n_rep
        return remote(req_out.at[peer], req_in.at[rep], req_send.at[step], req_recv.at[rep], peer, me)

    @pl.loop(1, n_rep)
    def _(step):
        req_copy(step).start()

    @pl.loop(1, n_rep)
    def _(step):
        sender = (rep + n_rep - step) % n_rep
        remote(req_out.at[sender], req_in.at[sender], req_send.at[step], req_recv.at[sender], sender, me).wait_recv()

    def row_copy(peer):
        return remote(
            picked.at[pl.ds(pl.multiple_of(peer * CAP, CAP), CAP)],
            fetched.at[pl.ds(pl.multiple_of(rep * CAP, CAP), CAP)],
            row_send.at[peer], row_recv.at[rep], peer, me,
        )

    groups = n_rep // per_tile

    @pl.loop(0, groups)
    def _(turn):
        group = (turn + rep // per_tile) % groups
        wanted = req_in[group * per_tile]
        for j in range(1, per_tile):
            wanted = wanted + req_in[group * per_tile + j]
        wanted_col = jnp.broadcast_to(wanted, (128, 128)).T[:, :1]
        hit = lax.broadcasted_iota(jnp.int32, (128, table.shape[0]), 1).astype(F32) + 1.0 == wanted_col
        picked[pl.ds(pl.multiple_of(group * 128, 128), 128)] = dot(
            jnp.where(hit, 1.0, 0.0).astype(BF16), table[...], NN
        ).astype(BF16)
        for j in range(per_tile):
            peer = group * per_tile + j

            @pl.when(peer != rep)
            def _():
                row_copy(peer).start()

    own_slots = pl.ds(pl.multiple_of(rep * CAP, CAP), CAP)
    fetched[own_slots] = picked[own_slots]

    h_wait(down, 0)
    ring_sends = [h_copy(6, down, 0, up), h_copy(7, down, 0, sibling)]
    for copy in ring_sends:
        copy.start()
    h_wait(up, 1)
    more = [h_copy(8, up, 1, down), h_copy(9, up, 1, sibling)]
    for copy in more:
        copy.start()
    ring_sends += more

    def turn_heads(owner):
        for b in range(heads_width // 256):
            block = heads[pl.ds(pl.multiple_of(owner * tokens, tokens), tokens), 256 * b : 256 * (b + 1)]
            heads_t[256 * b : 256 * (b + 1), pl.ds(pl.multiple_of(owner * tokens, tokens), tokens)] = block.T

    for copy in local:
        copy.wait()
    turn_heads(me)

    def turn_cot(owner):
        weighted_t[:, pl.ds(pl.multiple_of(owner * tokens, tokens), tokens)] = (
            cot[owner].astype(F32).T * gain_col[...]
        )

    turn_cot(me)

    h_wait(sibling, 0)
    h_wait(sibling, 1)
    turn_heads(sibling)

    h_wait(down, 1)
    h_wait(up, 0)
    more = [h_copy(10, down, 1, sibling), h_copy(11, up, 0, sibling)]
    for copy in more:
        copy.start()
    ring_sends += more
    turn_heads(down)
    turn_heads(up)

    @pl.loop(1, n_fsdp)
    def _(step):
        sender = (me + step) % n_fsdp
        remote(cot.at[sender], cot.at[sender], c_send.at[step], c_recv.at[sender], rep, sender).wait_recv()
        turn_cot(sender)

    other_up = (place + 1) % ring * 2 + 1 - core
    other_down = (place + ring - 1) % ring * 2 + 1 - core
    other_across = (place + 2) % ring * 2 + 1 - core
    for owner in (other_down, other_up):
        h_wait(owner, 0)
        h_wait(owner, 1)
        turn_heads(owner)
    for which in range(2):
        h_wait(across, which)
        copy = h_copy(12 + which, across, which, sibling)
        copy.start()
        ring_sends.append(copy)
    turn_heads(across)
    h_wait(other_across, 0)
    h_wait(other_across, 1)
    turn_heads(other_across)

    tile = 256
    for k in range(W_CHUNKS):
        w_copy(k).wait_recv()
        part = pl.ds(k * chunk, chunk)
        mixed = (w_own[part].astype(F32) + w_other[part].astype(F32)) * 0.5
        mixed_t[...] = mixed.T.astype(BF16)

        @pl.loop(0, all_tokens // tile)
        def _(i):
            where = pl.ds(pl.multiple_of(i * tile, tile), tile)
            part_sum = dot(mixed_t[...], heads[where, k * chunk : (k + 1) * chunk], NT)
            if k == 0:
                stream_t[:, where] = part_sum
            else:
                stream_t[:, where] += part_sum

    batch = 8
    span = batch * CAP

    @pl.loop(0, n_rep // batch)
    def _(g):
        for j in range(batch):
            v = g * batch + j

            @pl.when(v != rep)
            def _():
                slots = pl.ds(pl.multiple_of(v * CAP, CAP), CAP)
                remote(picked.at[slots], fetched.at[slots], row_send.at[v], row_recv.at[v], v, me).wait_recv()

        slots = pl.ds(pl.multiple_of(g * span, span), span)
        rows_t = fetched[slots].T
        for i in range(all_tokens // tile):
            where = slice(i * tile, (i + 1) * tile)
            slot = lax.broadcasted_iota(jnp.int32, (span, tile), 0) + g * span
            place_of = jnp.where(slot == position_row[:, where], 1.0, 0.0).astype(BF16)
            stream_t[:, where] += dot(rows_t, place_of, NN)

    stream = stream_t[...]
    stat_out[:, :all_tokens] = jnp.sum(stream * stream, axis=0, keepdims=True)
    stat_out[:, all_tokens:] = jnp.sum(stream * weighted_t[...], axis=0, keepdims=True)
    stat_in[me] = stat_out[...]

    def stat_copy(step):
        peer = (me + step) % n_fsdp
        return remote(stat_out, stat_in.at[me], stat_send.at[step], stat_recv.at[me], rep, peer)

    @pl.loop(1, n_fsdp)
    def _(step):
        stat_copy(step).start()

    @pl.loop(1, n_fsdp)
    def _(step):
        sender = (me + step) % n_fsdp
        remote(stat_out, stat_in.at[sender], stat_send.at[step], stat_recv.at[sender], rep, sender).wait_recv()

    total = stat_in[0]
    for j in range(1, n_fsdp):
        total = total + stat_in[j]
    total = total * (1.0 / features)
    inverse = 1.0 / jnp.sqrt(total[:, :all_tokens] + EPS)
    scale = total[:, all_tokens:] * inverse * inverse * inverse
    grad_t[...] = (weighted_t[...] * inverse - stream_t[...] * scale).astype(BF16)

    @pl.loop(0, rows // tile)
    def _(i):
        where = pl.ds(pl.multiple_of(i * tile, tile), tile)
        grad = dot(heads_t[where], grad_t[...], NT)
        mixed = (w_own[where].astype(F32) + w_other[where].astype(F32)) * 0.5
        out_ref[where] = (mixed - (RATE / all_tokens) * grad).astype(BF16)

    for copy in own_sends + ring_sends:
        copy.wait_send()
    for k in range(W_CHUNKS):
        w_copy(k).wait_send()

    @pl.loop(1, n_fsdp)
    def _(step):
        ids_copy(step).wait_send()
        c_copy(step).wait_send()
        stat_copy(step).wait_send()

    @pl.loop(1, n_rep)
    def _(step):
        req_copy(step).wait_send()
        row_copy((rep + step) % n_rep).wait_send()


def make_branch(level, n_rep, n_fsdp, weights, head_out, embed_table):
    rows, width = weights.shape
    tokens, heads_width = head_out.shape
    all_tokens = tokens * n_fsdp
    vocab_pad = -(-embed_table.shape[0] // 256) * 256
    dma = pltpu.SemaphoreType.DMA
    vmem = pl.BlockSpec(memory_space=pltpu.VMEM)
    hbm = pl.BlockSpec(memory_space=pl.ANY)
    slots = n_rep * CAP
    return pl.pallas_call(
        functools.partial(kernel, level, n_rep, n_fsdp),
        name=f"step_level_{level}",
        out_shape=jax.ShapeDtypeStruct((rows, width), BF16),
        in_specs=[vmem, hbm, hbm, hbm, vmem, vmem],
        out_specs=vmem,
        scratch_shapes=[
            pltpu.VMEM((n_fsdp, 1, tokens), jnp.int32),
            pltpu.VMEM((rows, width), BF16),
            pltpu.VMEM((rows, width), BF16),
            pltpu.VMEM((all_tokens, heads_width), BF16),
            pltpu.VMEM((heads_width, all_tokens), BF16),
            pltpu.VMEM((n_fsdp, tokens, width), BF16),
            pltpu.VMEM((width, all_tokens), F32),
            pltpu.VMEM((vocab_pad, width), BF16),
            pltpu.VMEM((n_rep, 1, 128), F32),
            pltpu.VMEM((n_rep, 1, 128), F32),
            pltpu.VMEM((slots, width), BF16),
            pltpu.VMEM((slots, width), BF16),
            pltpu.VMEM((width, rows // W_CHUNKS), BF16),
            pltpu.VMEM((width, all_tokens), F32),
            pltpu.VMEM((width, all_tokens), BF16),
            pltpu.VMEM((1, 2 * all_tokens), F32),
            pltpu.VMEM((n_fsdp, 1, 2 * all_tokens), F32),
            pltpu.VMEM((1, all_tokens), jnp.int32),
            pltpu.VMEM((width, 128), F32),
            dma((n_fsdp,)), dma((n_fsdp,)),
            dma((W_CHUNKS,)), dma((W_CHUNKS,)),
            dma((14,)), dma((n_fsdp, 2)),
            dma((n_fsdp,)), dma((n_fsdp,)),
            dma((n_rep,)), dma((n_rep,)),
            dma((n_rep,)), dma((n_rep,)),
            dma((n_fsdp,)), dma((n_fsdp,)),
            dma((3,)),
        ],
        compiler_params=pltpu.CompilerParams(
            collective_id=level, has_side_effects=True, vmem_limit_bytes=44 * 1024 * 1024
        ),
        cost_estimate=pl.CostEstimate(
            flops=6 * rows * width * all_tokens, bytes_accessed=8 * rows * width, transcendentals=all_tokens
        ),
    )


def local(weights, head_out, token_ids, embed_table, norm_gain, cotangent, mix_step):
    n_rep, n_fsdp = lax.axis_size("rep"), lax.axis_size("fsdp")
    branches = [
        make_branch(level, n_rep, n_fsdp, weights[0], head_out[0], embed_table) for level in range(MIXBITS)
    ]
    out = lax.switch(
        mix_step[0] % MIXBITS,
        branches,
        token_ids, weights[0], head_out[0], cotangent[0], embed_table, norm_gain[None],
    )
    return out[None]


def solution(mesh):
    return jax.shard_map(
        local,
        mesh=mesh,
        in_specs=(
            P("rep", None, "fsdp"),
            P("rep", "fsdp", None),
            P("rep", "fsdp"),
            P("rep", "fsdp"),
            P(),
            P("rep", "fsdp", None),
            P(),
        ),
        out_specs=P("rep", None, "fsdp"),
        check_vma=False,
    )
```

```python
import functools

import jax
import jax.numpy as jnp
from jax import lax
from jax.experimental import pallas as pl
from jax.experimental.pallas import tpu as pltpu
from jax.sharding import PartitionSpec as P

MIXBITS = 4
EPS = 1e-05
RATE = 0.5
CAP = 32
MESH = pl.DeviceIdType.MESH
F32 = jnp.float32
BF16 = jnp.bfloat16
W_CHUNKS = 8
W_FIRST = 2
W_NEXT = 2

NT = (((1,), (1,)), ((), ()))
NN = (((1,), (0,)), ((), ()))


def dot(a, b, dims):
    return lax.dot_general(a, b, dims, preferred_element_type=F32)


def kernel(
    level, n_rep, n_fsdp,
    ids_ref, w_ref, h_ref, c_ref, tab_ref, gain_ref, out_ref,
    ids_all, w_own, w_other, heads, heads_t, cot, weighted_t, table, req_out, req_in, picked, fetched, mixed_t,
    stream_t, grad_t, stat_out, stat_in, gain_col, place_of,
    ids_send, ids_recv, w_send, w_recv, h_send, h_recv, c_send, c_recv, req_send, req_recv, row_send, row_recv,
    stat_send, stat_recv, local_sem, out_sem,
):
    tokens, heads_width = h_ref.shape
    width = w_ref.shape[1]
    rows = w_ref.shape[0]
    features = width * n_fsdp
    all_tokens = tokens * n_fsdp
    vocab = tab_ref.shape[0]
    half = tokens // 2
    chunk = rows // W_CHUNKS
    rep = lax.axis_index("rep")
    me = lax.axis_index("fsdp")
    ring = n_fsdp // 2
    place, core = me // 2, me % 2
    up = (place + 1) % ring * 2 + core
    down = (place + ring - 1) % ring * 2 + core
    across = (place + 2) % ring * 2 + core
    sibling = place * 2 + 1 - core
    stride = 1 << level
    partner = rep + stride * (1 - 2 * (rep // stride % 2))

    def remote(src, dst, send, recv, r, f):
        return pltpu.make_async_remote_copy(
            src_ref=src, dst_ref=dst, send_sem=send, recv_sem=recv, device_id=(r, f), device_id_type=MESH
        )

    own_rows = pl.ds(pl.multiple_of(me * tokens, tokens), tokens)
    local = [
        pltpu.make_async_copy(w_ref, w_own, local_sem.at[0]),
        pltpu.make_async_copy(h_ref, heads.at[own_rows], local_sem.at[1]),
        pltpu.make_async_copy(
            c_ref.at[:, pl.ds(pl.multiple_of(me * width, width), width)], cot.at[me], local_sem.at[2]
        ),
    ]
    for copy in local:
        copy.start()

    barrier = pltpu.get_barrier_semaphore()

    @pl.loop(1, n_fsdp)
    def _(step):
        pl.semaphore_signal(barrier, inc=1, device_id=(rep, (me + step) % n_fsdp), device_id_type=MESH)

    @pl.loop(1, n_rep)
    def _(step):
        pl.semaphore_signal(barrier, inc=1, device_id=((rep + step) % n_rep, me), device_id_type=MESH)

    ids_all[me] = ids_ref[...]
    table[...] = jnp.zeros_like(table)
    table[:vocab] = tab_ref[...]
    gain = gain_ref[:, pl.ds(pl.multiple_of(me * width, width), width)]
    gain_col[...] = jnp.broadcast_to(gain, (128, width)).T

    pl.semaphore_wait(barrier, n_fsdp - 1 + n_rep - 1)

    def ids_copy(step):
        peer = (me + step) % n_fsdp
        return remote(ids_all.at[me], ids_all.at[me], ids_send.at[step], ids_recv.at[me], rep, peer)

    @pl.loop(1, n_fsdp)
    def _(step):
        ids_copy(step).start()

    def w_copy(k):
        part = pl.ds(k * chunk, chunk)
        return remote(w_ref.at[part], w_other.at[part], w_send.at[k], w_recv.at[k], partner, me)

    for k in range(W_FIRST):
        w_copy(k).start()

    def part_rows(owner, which):
        return pl.ds(pl.multiple_of(owner * tokens + which * half, half), half)

    def h_copy(index, owner, which, target, own=False):
        src = h_ref.at[pl.ds(which * half, half)] if own else heads.at[part_rows(owner, which)]
        return remote(
            src, heads.at[part_rows(owner, which)], h_send.at[index], h_recv.at[owner, which], rep, target
        )

    def h_wait(owner, which):
        h_copy(0, owner, which, sibling).wait_recv()

    own_sends = [
        h_copy(0, me, 0, up, True),
        h_copy(1, me, 1, down, True),
        h_copy(2, me, 1, up, True),
        h_copy(3, me, 0, down, True),
        h_copy(4, me, 0, sibling, True),
        h_copy(5, me, 1, sibling, True),
    ]
    for copy in own_sends[:2]:
        copy.start()

    def c_copy(step):
        peer = (me + step) % n_fsdp
        return remote(
            c_ref.at[:, pl.ds(pl.multiple_of(peer * width, width), width)],
            cot.at[me], c_send.at[step], c_recv.at[me], rep, peer,
        )

    earlier = jnp.where(
        lax.broadcasted_iota(jnp.int32, (tokens, tokens), 0) < lax.broadcasted_iota(jnp.int32, (tokens, tokens), 1),
        1.0,
        0.0,
    ).astype(BF16)

    def start_c():
        @pl.loop(1, n_fsdp)
        def _(step):
            c_copy(step).start()

    ring_sends = []

    def pass_on(*copies):
        for copy in copies:
            copy.start()
            ring_sends.append(copy)

    def forward():
        h_wait(down, 0)
        pass_on(h_copy(6, down, 0, up), h_copy(7, down, 0, sibling))
        h_wait(up, 1)
        pass_on(h_copy(8, up, 1, down), h_copy(9, up, 1, sibling))

    @pl.loop(1, n_fsdp)
    def _(step):
        sender = (me + step) % n_fsdp
        remote(ids_all.at[me], ids_all.at[sender], ids_send.at[step], ids_recv.at[sender], rep, sender).wait_recv()

    ids_row = jnp.concatenate([ids_all[j] for j in range(n_fsdp)], axis=1)
    owner_row = ids_row // vocab
    local_row = ids_row - owner_row * vocab + 1
    block_iota = lax.broadcasted_iota(jnp.int32, (n_rep, all_tokens), 0)
    owned = block_iota == owner_row
    owned_b = jnp.where(owned, 1.0, 0.0).astype(BF16)
    ranks = []
    seen = jnp.zeros((n_rep, 1), F32)
    for j in range(n_fsdp):
        part = slice(j * tokens, (j + 1) * tokens)
        before = dot(owned_b[:, part], earlier, NN) + seen
        ranks.append(jnp.sum(jnp.where(owned[:, part], before, 0.0), axis=0, keepdims=True))
        seen = seen + jnp.sum(jnp.where(owned[:, part], 1.0, 0.0), axis=1, keepdims=True)
    rank = jnp.concatenate(ranks, axis=1).astype(jnp.int32)
    position = owner_row * CAP + rank
    per_tile = 128 // CAP
    lane = rank + rep % per_tile * CAP
    here = lax.broadcasted_iota(jnp.int32, (128, all_tokens), 0) == lane
    high = jnp.where(here, (local_row // 2).astype(F32), 0.0).astype(BF16)
    low = jnp.where(here, (local_row % 2).astype(F32), 0.0).astype(BF16)
    counted = dot(owned_b, jnp.concatenate([high, low], axis=0), NT)
    requests = counted[:, :128] * 2.0 + counted[:, 128:]
    for v in range(n_rep):
        req_out[v] = requests[v : v + 1]
    req_in[rep] = req_out[rep]

    pair = 2 * per_tile
    pairs = n_rep // pair

    def req_copy(step):
        peer = (rep // pair + step // pair) % pairs * pair + (rep + step) % pair
        return remote(req_out.at[peer], req_in.at[rep], req_send.at[step], req_recv.at[rep], peer, me)

    @pl.loop(1, n_rep)
    def _(step):
        req_copy(step).start()

    for k in range(W_FIRST, W_FIRST + W_NEXT):
        w_copy(k).start()

    for copy in own_sends[2:]:
        copy.start()
    start_c()
    forward()

    def row_copy(peer):
        return remote(
            picked.at[pl.ds(pl.multiple_of(peer * CAP, CAP), CAP)],
            fetched.at[pl.ds(pl.multiple_of(rep * CAP, CAP), CAP)],
            row_send.at[peer], row_recv.at[rep], peer, me,
        )

    @pl.loop(0, pairs)
    def _(turn):
        first = (rep // pair + pairs - turn) % pairs * pair
        for j in range(pair):
            sender = first + (rep + j) % pair

            @pl.when(sender != rep)
            def _():
                remote(
                    req_out.at[sender], req_in.at[sender], req_send.at[0], req_recv.at[sender], sender, me
                ).wait_recv()

        columns = []
        for g in range(2):
            wanted = req_in[first + g * per_tile]
            for j in range(1, per_tile):
                wanted = wanted + req_in[first + g * per_tile + j]
            columns.append(jnp.broadcast_to(wanted, (8, 128)).T[:, :1])
        wanted_col = jnp.concatenate(columns, axis=0)
        hit = lax.broadcasted_iota(jnp.int32, (256, table.shape[0]), 1).astype(F32) + 1.0 == wanted_col
        picked[pl.ds(pl.multiple_of(first * CAP, 256), 256)] = dot(
            jnp.where(hit, 1.0, 0.0).astype(BF16), table[...], NN
        ).astype(BF16)
        for j in range(pair):
            peer = first + (rep + j) % pair

            @pl.when(peer != rep)
            def _():
                row_copy(peer).start()

    for k in range(W_FIRST + W_NEXT, W_CHUNKS):
        w_copy(k).start()

    own_slots = pl.ds(pl.multiple_of(rep * CAP, CAP), CAP)
    fetched[own_slots] = picked[own_slots]

    tile = 256
    for copy in local:
        copy.wait()

    @pl.loop(0, n_rep * CAP // tile)
    def _(i):
        slot = lax.broadcasted_iota(jnp.int32, (tile, all_tokens), 0) + i * tile
        place_of[pl.ds(pl.multiple_of(i * tile, tile), tile)] = jnp.where(slot == position, 1.0, 0.0).astype(BF16)

    def token_rows(owner):
        return pl.ds(pl.multiple_of(owner * tokens, tokens), tokens)

    def turn_heads(owner):
        for b in range(heads_width // 256):
            heads_t[256 * b : 256 * (b + 1), token_rows(owner)] = heads[
                token_rows(owner), 256 * b : 256 * (b + 1)
            ].T

    def turn_cot(owner):
        weighted_t[:, token_rows(owner)] = cot[owner].astype(F32).T * gain_col[...]

    def embed(begin, end):
        @pl.loop(begin, end)
        def _(turn):
            first = (rep // pair + turn) % pairs * pair
            for j in range(pair):
                v = first + j

                @pl.when(v != rep)
                def _():
                    slots = pl.ds(pl.multiple_of(v * CAP, CAP), CAP)
                    remote(
                        picked.at[slots], fetched.at[slots], row_send.at[v], row_recv.at[v], v, me
                    ).wait_recv()

            slots = pl.ds(pl.multiple_of(first * CAP, pair * CAP), pair * CAP)
            rows_t = fetched[slots].T
            stream_t[...] += dot(rows_t, place_of[slots], NN)

    def mix(k):
        w_copy(k).wait_recv()
        part = pl.ds(k * chunk, chunk)
        mixed = (w_own[part].astype(F32) + w_other[part].astype(F32)) * 0.5
        mixed_t[:, part] = mixed.astype(BF16).T

    def project(k, count=1):
        part = slice(k * chunk, (k + count) * chunk)
        stream_t[...] += dot(mixed_t[:, part], heads_t[part], NN)

    def project_place(at):
        where = pl.ds(pl.multiple_of(at * 2 * tokens, 2 * tokens), 2 * tokens)
        stream_t[:, where] += dot(mixed_t[...], heads_t[:, where], NN)

    other_up = (place + 1) % ring * 2 + 1 - core
    other_down = (place + ring - 1) % ring * 2 + 1 - core
    other_across = (place + 2) % ring * 2 + 1 - core

    def finish_sends():
        @pl.loop(1, n_fsdp)
        def _(step):
            ids_copy(step).wait_send()
            c_copy(step).wait_send()

        @pl.loop(1, n_rep)
        def _(step):
            req_copy(step).wait_send()
            row_copy((rep + step) % n_rep).wait_send()

        for k in range(W_CHUNKS):
            w_copy(k).wait_send()

    stream_t[...] = jnp.zeros_like(stream_t)
    turn_heads(me)
    turn_cot(me)
    h_wait(sibling, 0)
    h_wait(sibling, 1)
    turn_heads(sibling)
    h_wait(down, 1)
    h_wait(up, 0)
    pass_on(h_copy(10, down, 1, sibling), h_copy(11, up, 0, sibling))
    turn_heads(down)
    turn_heads(up)
    for owner in (other_down, other_up):
        h_wait(owner, 0)
        h_wait(owner, 1)
        turn_heads(owner)

    @pl.loop(1, n_fsdp)
    def _(step):
        sender = (me + step) % n_fsdp
        remote(cot.at[sender], cot.at[sender], c_send.at[step], c_recv.at[sender], rep, sender).wait_recv()
        turn_cot(sender)

    def take_across():
        for which in range(2):
            h_wait(across, which)
            pass_on(h_copy(12 + which, across, which, sibling))
        turn_heads(across)
        h_wait(other_across, 0)
        h_wait(other_across, 1)
        turn_heads(other_across)

    late = pairs - 2
    early = W_FIRST + W_NEXT
    if level == 0:
        for k in range(W_CHUNKS):
            mix(k)
        for step in (0, 1, ring - 1):
            project_place((place + step) % ring)
        embed(0, late)
        take_across()
        project_place((place + 2) % ring)
        finish_sends()
        embed(late, pairs)
    else:
        for k in range(early):
            mix(k)
        embed(0, late)
        take_across()
        project(0, early)
        embed(late, pairs)
        for k in range(early, W_CHUNKS - 1):
            mix(k)
            project(k)
        finish_sends()
        mix(W_CHUNKS - 1)
        project(W_CHUNKS - 1)

    stream = stream_t[...]
    stat_out[:, :all_tokens] = jnp.sum(stream * stream, axis=0, keepdims=True)
    stat_out[:, all_tokens:] = jnp.sum(stream * weighted_t[...], axis=0, keepdims=True)

    def stat_copy(step):
        peer = (me + step) % n_fsdp
        return remote(stat_out, stat_in.at[me], stat_send.at[step], stat_recv.at[me], rep, peer)

    for step in range(1, n_fsdp):
        stat_copy(step).start()
    stat_in[me] = stat_out[...]
    for step in range(1, n_fsdp):
        sender = (me + step) % n_fsdp
        remote(stat_out, stat_in.at[sender], stat_send.at[step], stat_recv.at[sender], rep, sender).wait_recv()

    total = stat_in[0]
    for j in range(1, n_fsdp):
        total = total + stat_in[j]
    total = total * (1.0 / features)
    inverse = 1.0 / jnp.sqrt(total[:, :all_tokens] + EPS)
    scale = total[:, all_tokens:] * inverse * inverse * inverse
    grad_t[...] = (weighted_t[...] * inverse - stream_t[...] * scale).astype(BF16)

    @pl.loop(0, rows // (2 * tile))
    def _(i):
        where = pl.ds(pl.multiple_of(i * 2 * tile, 2 * tile), 2 * tile)
        grad = dot(heads_t[where], grad_t[...], NT)
        mixed = (w_own[where].astype(F32) + w_other[where].astype(F32)) * 0.5
        w_own[where] = (mixed - (RATE / all_tokens) * grad).astype(BF16)
        pltpu.make_async_copy(w_own.at[where], out_ref.at[where], out_sem.at[i]).start()

    for i in range(rows // (2 * tile)):
        where = pl.ds(i * 2 * tile, 2 * tile)
        pltpu.make_async_copy(w_own.at[where], out_ref.at[where], out_sem.at[i]).wait()
    for copy in own_sends + ring_sends:
        copy.wait_send()
    for step in range(1, n_fsdp):
        stat_copy(step).wait_send()


def make_branch(level, n_rep, n_fsdp, weights, head_out, embed_table):
    rows, width = weights.shape
    tokens, heads_width = head_out.shape
    all_tokens = tokens * n_fsdp
    vocab_pad = -(-embed_table.shape[0] // 256) * 256
    dma = pltpu.SemaphoreType.DMA
    vmem = pl.BlockSpec(memory_space=pltpu.VMEM)
    hbm = pl.BlockSpec(memory_space=pl.ANY)
    slots = n_rep * CAP
    return pl.pallas_call(
        functools.partial(kernel, level, n_rep, n_fsdp),
        name=f"step_level_{level}",
        out_shape=jax.ShapeDtypeStruct((rows, width), BF16),
        in_specs=[vmem, hbm, hbm, hbm, vmem, vmem],
        out_specs=hbm,
        scratch_shapes=[
            pltpu.VMEM((n_fsdp, 1, tokens), jnp.int32),
            pltpu.VMEM((rows, width), BF16),
            pltpu.VMEM((rows, width), BF16),
            pltpu.VMEM((all_tokens, heads_width), BF16),
            pltpu.VMEM((heads_width, all_tokens), BF16),
            pltpu.VMEM((n_fsdp, tokens, width), BF16),
            pltpu.VMEM((width, all_tokens), F32),
            pltpu.VMEM((vocab_pad, width), BF16),
            pltpu.VMEM((n_rep, 1, 128), F32),
            pltpu.VMEM((n_rep, 1, 128), F32),
            pltpu.VMEM((slots, width), BF16),
            pltpu.VMEM((slots, width), BF16),
            pltpu.VMEM((width, rows), BF16),
            pltpu.VMEM((width, all_tokens), F32),
            pltpu.VMEM((width, all_tokens), BF16),
            pltpu.VMEM((1, 2 * all_tokens), F32),
            pltpu.VMEM((n_fsdp, 1, 2 * all_tokens), F32),
            pltpu.VMEM((width, 128), F32),
            pltpu.VMEM((slots, all_tokens), BF16),
            dma((n_fsdp,)), dma((n_fsdp,)),
            dma((W_CHUNKS,)), dma((W_CHUNKS,)),
            dma((14,)), dma((n_fsdp, 2)),
            dma((n_fsdp,)), dma((n_fsdp,)),
            dma((n_rep,)), dma((n_rep,)),
            dma((n_rep,)), dma((n_rep,)),
            dma((n_fsdp,)), dma((n_fsdp,)),
            dma((3,)), dma((rows // 512,)),
        ],
        compiler_params=pltpu.CompilerParams(
            collective_id=level, has_side_effects=True, vmem_limit_bytes=44 * 1024 * 1024
        ),
        cost_estimate=pl.CostEstimate(
            flops=6 * rows * width * all_tokens, bytes_accessed=8 * rows * width, transcendentals=all_tokens
        ),
    )


def local(weights, head_out, token_ids, embed_table, norm_gain, cotangent, mix_step):
    n_rep, n_fsdp = lax.axis_size("rep"), lax.axis_size("fsdp")
    branches = [
        make_branch(level, n_rep, n_fsdp, weights[0], head_out[0], embed_table) for level in range(MIXBITS)
    ]
    out = lax.switch(
        mix_step[0] % MIXBITS,
        branches,
        token_ids, weights[0], head_out[0], cotangent[0], embed_table, norm_gain[None],
    )
    return out[None]


def solution(mesh):
    return jax.shard_map(
        local,
        mesh=mesh,
        in_specs=(
            P("rep", None, "fsdp"),
            P("rep", "fsdp", None),
            P("rep", "fsdp"),
            P("rep", "fsdp"),
            P(),
            P("rep", "fsdp", None),
            P(),
        ),
        out_specs=P("rep", None, "fsdp"),
        check_vma=False,
    )
```

```python
import functools

import jax
import jax.numpy as jnp
from jax import lax
from jax.experimental import pallas as pl
from jax.experimental.pallas import tpu as pltpu
from jax.sharding import PartitionSpec as P

MIXBITS = 4
EPS = 1e-05
RATE = 0.5
PLACES = 8
CAP = 32
MESH = pl.DeviceIdType.MESH
F32 = jnp.float32
BF16 = jnp.bfloat16
W_CHUNKS = 8
W_SENT = ((2, 6), (3, 3), (3, 3), (3, 3))

NT = (((1,), (1,)), ((), ()))
NN = (((1,), (0,)), ((), ()))


def dot(a, b, dims):
    return lax.dot_general(a, b, dims, preferred_element_type=F32)


def kernel(
    level, n_rep, n_fsdp,
    ids_ref, w_ref, h_ref, c_ref, tab_ref, gain_ref, out_ref,
    ids_all, w_own, w_other, heads, heads_t, cot, weighted_t, table, req_out, req_in, picked, fetched, mixed_t,
    stream_t, grad_t, stat_out, stat_in, gain_col, place_of,
    ids_send, ids_recv, w_send, w_recv, h_send, h_recv, c_send, c_recv, req_send, req_recv, row_send, row_recv,
    stat_send, stat_recv, local_sem, out_sem, table_send, table_recv,
):
    tokens, heads_width = h_ref.shape
    width = w_ref.shape[1]
    rows = w_ref.shape[0]
    features = width * n_fsdp
    all_tokens = tokens * n_fsdp
    vocab = tab_ref.shape[0]
    half = tokens // 2
    chunk = rows // W_CHUNKS
    rep = lax.axis_index("rep")
    me = lax.axis_index("fsdp")
    ring = n_fsdp // 2
    place, core = me // 2, me % 2
    up = (place + 1) % ring * 2 + core
    down = (place + ring - 1) % ring * 2 + core
    across = (place + 2) % ring * 2 + core
    sibling = place * 2 + 1 - core
    side = rep // PLACES % 2
    across_z = rep + PLACES * (1 - 2 * side)
    n_peers = n_rep // 2
    my = rep // (2 * PLACES) * PLACES + rep % PLACES

    def replica(index):
        return index // PLACES * (2 * PLACES) + side * PLACES + index % PLACES

    stride = 1 << level
    w_first, w_next = W_SENT[level]
    partner = rep + stride * (1 - 2 * (rep // stride % 2))

    def remote(src, dst, send, recv, r, f):
        return pltpu.make_async_remote_copy(
            src_ref=src, dst_ref=dst, send_sem=send, recv_sem=recv, device_id=(r, f), device_id_type=MESH
        )

    own_rows = pl.ds(pl.multiple_of(me * tokens, tokens), tokens)
    local = [
        pltpu.make_async_copy(w_ref, w_own, local_sem.at[0]),
        pltpu.make_async_copy(h_ref, heads.at[own_rows], local_sem.at[1]),
        pltpu.make_async_copy(
            c_ref.at[:, pl.ds(pl.multiple_of(me * width, width), width)], cot.at[me], local_sem.at[2]
        ),
    ]
    for copy in local:
        copy.start()

    barrier = pltpu.get_barrier_semaphore()

    @pl.loop(1, n_fsdp)
    def _(step):
        pl.semaphore_signal(barrier, inc=1, device_id=(rep, (me + step) % n_fsdp), device_id_type=MESH)

    @pl.loop(1, n_peers)
    def _(step):
        pl.semaphore_signal(barrier, inc=1, device_id=(replica((my + step) % n_peers), me), device_id_type=MESH)

    pl.semaphore_signal(barrier, inc=1, device_id=(across_z, me), device_id_type=MESH)

    ids_all[me] = ids_ref[...]
    table[side] = jnp.zeros(table.shape[1:], BF16)
    table[side, :vocab] = tab_ref[...]
    gain = gain_ref[:, pl.ds(pl.multiple_of(me * width, width), width)]
    gain_col[...] = jnp.broadcast_to(gain, (128, width)).T

    pl.semaphore_wait(barrier, n_fsdp - 1 + n_peers)

    def ids_copy(step):
        peer = (me + step) % n_fsdp
        return remote(ids_all.at[me], ids_all.at[me], ids_send.at[step], ids_recv.at[me], rep, peer)

    @pl.loop(1, n_fsdp)
    def _(step):
        ids_copy(step).start()

    table_copy = remote(table.at[side], table.at[side], table_send.at[0], table_recv.at[0], across_z, me)
    table_copy.start()

    def w_copy(k):
        part = pl.ds(k * chunk, chunk)
        return remote(w_ref.at[part], w_other.at[part], w_send.at[k], w_recv.at[k], partner, me)

    for k in range(w_first):
        w_copy(k).start()

    def part_rows(owner, which):
        return pl.ds(pl.multiple_of(owner * tokens + which * half, half), half)

    def h_copy(index, owner, which, target, own=False):
        src = h_ref.at[pl.ds(which * half, half)] if own else heads.at[part_rows(owner, which)]
        return remote(
            src, heads.at[part_rows(owner, which)], h_send.at[index], h_recv.at[owner, which], rep, target
        )

    def h_wait(owner, which):
        h_copy(0, owner, which, sibling).wait_recv()

    own_sends = [
        h_copy(0, me, 0, up, True),
        h_copy(1, me, 1, down, True),
        h_copy(2, me, 1, up, True),
        h_copy(3, me, 0, down, True),
        h_copy(4, me, 0, sibling, True),
        h_copy(5, me, 1, sibling, True),
    ]
    for copy in own_sends[:2]:
        copy.start()

    def c_copy(step):
        peer = (me + step) % n_fsdp
        return remote(
            c_ref.at[:, pl.ds(pl.multiple_of(peer * width, width), width)],
            cot.at[me], c_send.at[step], c_recv.at[me], rep, peer,
        )

    earlier = jnp.where(
        lax.broadcasted_iota(jnp.int32, (tokens, tokens), 0) < lax.broadcasted_iota(jnp.int32, (tokens, tokens), 1),
        1.0,
        0.0,
    ).astype(BF16)

    def start_c():
        @pl.loop(1, n_fsdp)
        def _(step):
            c_copy(step).start()

    ring_sends = []

    def pass_on(*copies):
        for copy in copies:
            copy.start()
            ring_sends.append(copy)

    def forward():
        h_wait(down, 0)
        pass_on(h_copy(6, down, 0, up), h_copy(7, down, 0, sibling))
        h_wait(up, 1)
        pass_on(h_copy(8, up, 1, down), h_copy(9, up, 1, sibling))

    @pl.loop(1, n_fsdp)
    def _(step):
        sender = (me + step) % n_fsdp
        remote(ids_all.at[me], ids_all.at[sender], ids_send.at[step], ids_recv.at[sender], rep, sender).wait_recv()

    ids_row = jnp.concatenate([ids_all[j] for j in range(n_fsdp)], axis=1)
    owner_row = ids_row // vocab
    local_row = ids_row - owner_row * vocab + 1
    block_iota = lax.broadcasted_iota(jnp.int32, (n_rep, all_tokens), 0)
    owned = block_iota == owner_row
    owned_b = jnp.where(owned, 1.0, 0.0).astype(BF16)
    ranks = []
    seen = jnp.zeros((n_rep, 1), F32)
    for j in range(n_fsdp):
        part = slice(j * tokens, (j + 1) * tokens)
        before = dot(owned_b[:, part], earlier, NN) + seen
        ranks.append(jnp.sum(jnp.where(owned[:, part], before, 0.0), axis=0, keepdims=True))
        seen = seen + jnp.sum(jnp.where(owned[:, part], 1.0, 0.0), axis=1, keepdims=True)
    rank = jnp.concatenate(ranks, axis=1).astype(jnp.int32)
    owner_side = owner_row // PLACES % 2
    owner_peer = owner_row // (2 * PLACES) * PLACES + owner_row % PLACES
    position = (owner_peer * 2 + owner_side) * CAP + rank
    asked = lax.broadcasted_iota(jnp.int32, (n_peers, all_tokens), 0) == owner_peer
    asked_b = jnp.where(asked, 1.0, 0.0).astype(BF16)
    lane = (owner_side * 2 + my % 2) * CAP + rank
    here = lax.broadcasted_iota(jnp.int32, (128, all_tokens), 0) == lane
    high = jnp.where(here, (local_row // 2).astype(F32), 0.0).astype(BF16)
    low = jnp.where(here, (local_row % 2).astype(F32), 0.0).astype(BF16)
    counted = dot(asked_b, jnp.concatenate([high, low], axis=0), NT)
    requests = counted[:, :128] * 2.0 + counted[:, 128:]
    for v in range(n_peers):
        req_out[v] = requests[v : v + 1]
    req_in[my] = req_out[my]

    pair = PLACES
    pairs = n_peers // pair

    def req_copy(step):
        peer = (my // pair + step // pair) % pairs * pair + (my + step) % pair
        return remote(req_out.at[peer], req_in.at[my], req_send.at[step], req_recv.at[my], replica(peer), me)

    @pl.loop(1, n_peers)
    def _(step):
        req_copy(step).start()

    for k in range(w_first, w_first + w_next):
        w_copy(k).start()

    for copy in own_sends[2:]:
        copy.start()
    start_c()
    forward()

    def peer_slots(peer):
        return pl.ds(pl.multiple_of(peer * 2 * CAP, 2 * CAP), 2 * CAP)

    def row_copy(peer):
        return remote(
            picked.at[peer_slots(peer)], fetched.at[peer_slots(my)],
            row_send.at[peer], row_recv.at[my], replica(peer), me,
        )

    table_other = table.at[1 - side]
    remote(table_other, table_other, table_send.at[0], table_recv.at[0], across_z, me).wait_recv()

    @pl.loop(0, pairs)
    def _(turn):
        first = (my // pair + pairs - turn) % pairs * pair
        for j in range(pair):
            sender = first + (my + j) % pair

            @pl.when(sender != my)
            def _():
                remote(
                    req_out.at[sender], req_in.at[sender], req_send.at[0], req_recv.at[sender], replica(sender), me
                ).wait_recv()

        columns = []
        for g in range(pair // 2):
            wanted = req_in[first + 2 * g] + req_in[first + 2 * g + 1]
            columns.append(jnp.broadcast_to(wanted, (8, 128)).T[:, :1])
        row_iota = lax.broadcasted_iota(jnp.int32, (pair * CAP, table.shape[1]), 1).astype(F32) + 1.0
        for b in range(2):
            wanted_col = jnp.concatenate([c[b * 2 * CAP : (b + 1) * 2 * CAP] for c in columns], axis=0)
            found = dot(jnp.where(row_iota == wanted_col, 1.0, 0.0).astype(BF16), table[b], NN).astype(BF16)
            for j in range(pair):
                slots = pl.ds(pl.multiple_of((first + j) * 2 * CAP + b * CAP, CAP), CAP)
                picked[slots] = found[j * CAP : (j + 1) * CAP]
        for j in range(pair):
            peer = first + (my + j) % pair

            @pl.when(peer != my)
            def _():
                row_copy(peer).start()

    for k in range(w_first + w_next, W_CHUNKS):
        w_copy(k).start()

    fetched[peer_slots(my)] = picked[peer_slots(my)]

    tile = 256
    for copy in local:
        copy.wait()

    @pl.loop(0, n_rep * CAP // tile)
    def _(i):
        slot = lax.broadcasted_iota(jnp.int32, (tile, all_tokens), 0) + i * tile
        place_of[pl.ds(pl.multiple_of(i * tile, tile), tile)] = jnp.where(slot == position, 1.0, 0.0).astype(BF16)

    def token_rows(owner):
        return pl.ds(pl.multiple_of(owner * tokens, tokens), tokens)

    def turn_heads(owner):
        for b in range(heads_width // 256):
            heads_t[256 * b : 256 * (b + 1), token_rows(owner)] = heads[
                token_rows(owner), 256 * b : 256 * (b + 1)
            ].T

    def turn_cot(owner):
        weighted_t[:, token_rows(owner)] = cot[owner].astype(F32).T * gain_col[...]

    def embed(begin, end):
        @pl.loop(begin, end)
        def _(turn):
            first = (my // pair + turn) % pairs * pair
            for j in range(pair):
                v = first + j

                @pl.when(v != my)
                def _():
                    remote(
                        picked.at[peer_slots(v)], fetched.at[peer_slots(v)],
                        row_send.at[v], row_recv.at[v], replica(v), me,
                    ).wait_recv()

            slots = pl.ds(pl.multiple_of(first * 2 * CAP, pair * 2 * CAP), pair * 2 * CAP)
            rows_t = fetched[slots].T
            stream_t[...] += dot(rows_t, place_of[slots], NN)

    def mix(k):
        w_copy(k).wait_recv()
        part = pl.ds(k * chunk, chunk)
        mixed = (w_own[part].astype(F32) + w_other[part].astype(F32)) * 0.5
        mixed_t[:, part] = mixed.astype(BF16).T

    def project(k, count=1):
        part = slice(k * chunk, (k + count) * chunk)
        stream_t[...] += dot(mixed_t[:, part], heads_t[part], NN)

    def project_place(at):
        where = pl.ds(pl.multiple_of(at * 2 * tokens, 2 * tokens), 2 * tokens)
        stream_t[:, where] += dot(mixed_t[...], heads_t[:, where], NN)

    other_up = (place + 1) % ring * 2 + 1 - core
    other_down = (place + ring - 1) % ring * 2 + 1 - core
    other_across = (place + 2) % ring * 2 + 1 - core

    def finish_sends():
        @pl.loop(1, n_fsdp)
        def _(step):
            ids_copy(step).wait_send()
            c_copy(step).wait_send()

        table_copy.wait_send()

        @pl.loop(1, n_peers)
        def _(step):
            req_copy(step).wait_send()
            row_copy((my + step) % n_peers).wait_send()

        for k in range(W_CHUNKS):
            w_copy(k).wait_send()

    stream_t[...] = jnp.zeros_like(stream_t)
    turn_heads(me)
    turn_cot(me)
    h_wait(sibling, 0)
    h_wait(sibling, 1)
    turn_heads(sibling)
    h_wait(down, 1)
    h_wait(up, 0)
    pass_on(h_copy(10, down, 1, sibling), h_copy(11, up, 0, sibling))
    turn_heads(down)
    turn_heads(up)
    for owner in (other_down, other_up):
        h_wait(owner, 0)
        h_wait(owner, 1)
        turn_heads(owner)

    @pl.loop(1, n_fsdp)
    def _(step):
        sender = (me + step) % n_fsdp
        remote(cot.at[sender], cot.at[sender], c_send.at[step], c_recv.at[sender], rep, sender).wait_recv()
        turn_cot(sender)

    def take_across():
        for which in range(2):
            h_wait(across, which)
            pass_on(h_copy(12 + which, across, which, sibling))
        turn_heads(across)
        h_wait(other_across, 0)
        h_wait(other_across, 1)
        turn_heads(other_across)

    late = pairs - 1
    early = w_first + w_next
    if level == 0:
        for k in range(W_CHUNKS):
            mix(k)
        for step in (0, 1, ring - 1):
            project_place((place + step) % ring)
        embed(0, late)
        take_across()
        project_place((place + 2) % ring)
        finish_sends()
        embed(late, pairs)
    else:
        for k in range(early):
            mix(k)
        embed(0, late)
        take_across()
        project(0, early)
        embed(late, pairs)
        for k in range(early, W_CHUNKS - 1):
            mix(k)
            project(k)
        finish_sends()
        mix(W_CHUNKS - 1)
        project(W_CHUNKS - 1)

    stream = stream_t[...]
    stat_out[:, :all_tokens] = jnp.sum(stream * stream, axis=0, keepdims=True)
    stat_out[:, all_tokens:] = jnp.sum(stream * weighted_t[...], axis=0, keepdims=True)

    def stat_copy(step):
        peer = (me + step) % n_fsdp
        return remote(stat_out, stat_in.at[me], stat_send.at[step], stat_recv.at[me], rep, peer)

    for step in range(1, n_fsdp):
        stat_copy(step).start()
    stat_in[me] = stat_out[...]
    for step in range(1, n_fsdp):
        sender = (me + step) % n_fsdp
        remote(stat_out, stat_in.at[sender], stat_send.at[step], stat_recv.at[sender], rep, sender).wait_recv()

    total = stat_in[0]
    for j in range(1, n_fsdp):
        total = total + stat_in[j]
    total = total * (1.0 / features)
    inverse = 1.0 / jnp.sqrt(total[:, :all_tokens] + EPS)
    scale = total[:, all_tokens:] * inverse * inverse * inverse
    grad_t[...] = (weighted_t[...] * inverse - stream_t[...] * scale).astype(BF16)

    @pl.loop(0, rows // (2 * tile))
    def _(i):
        where = pl.ds(pl.multiple_of(i * 2 * tile, 2 * tile), 2 * tile)
        grad = dot(heads_t[where], grad_t[...], NT)
        mixed = (w_own[where].astype(F32) + w_other[where].astype(F32)) * 0.5
        w_own[where] = (mixed - (RATE / all_tokens) * grad).astype(BF16)
        pltpu.make_async_copy(w_own.at[where], out_ref.at[where], out_sem.at[i]).start()

    for i in range(rows // (2 * tile)):
        where = pl.ds(i * 2 * tile, 2 * tile)
        pltpu.make_async_copy(w_own.at[where], out_ref.at[where], out_sem.at[i]).wait()
    for copy in own_sends + ring_sends:
        copy.wait_send()
    for step in range(1, n_fsdp):
        stat_copy(step).wait_send()


def make_branch(level, n_rep, n_fsdp, weights, head_out, embed_table):
    rows, width = weights.shape
    tokens, heads_width = head_out.shape
    all_tokens = tokens * n_fsdp
    vocab_pad = -(-embed_table.shape[0] // 256) * 256
    dma = pltpu.SemaphoreType.DMA
    vmem = pl.BlockSpec(memory_space=pltpu.VMEM)
    hbm = pl.BlockSpec(memory_space=pl.ANY)
    slots = n_rep * CAP
    return pl.pallas_call(
        functools.partial(kernel, level, n_rep, n_fsdp),
        name=f"step_level_{level}",
        out_shape=jax.ShapeDtypeStruct((rows, width), BF16),
        in_specs=[vmem, hbm, hbm, hbm, vmem, vmem],
        out_specs=hbm,
        scratch_shapes=[
            pltpu.VMEM((n_fsdp, 1, tokens), jnp.int32),
            pltpu.VMEM((rows, width), BF16),
            pltpu.VMEM((rows, width), BF16),
            pltpu.VMEM((all_tokens, heads_width), BF16),
            pltpu.VMEM((heads_width, all_tokens), BF16),
            pltpu.VMEM((n_fsdp, tokens, width), BF16),
            pltpu.VMEM((width, all_tokens), F32),
            pltpu.VMEM((2, vocab_pad, width), BF16),
            pltpu.VMEM((n_rep // 2, 1, 128), F32),
            pltpu.VMEM((n_rep // 2, 1, 128), F32),
            pltpu.VMEM((slots, width), BF16),
            pltpu.VMEM((slots, width), BF16),
            pltpu.VMEM((width, rows), BF16),
            pltpu.VMEM((width, all_tokens), F32),
            pltpu.VMEM((width, all_tokens), BF16),
            pltpu.VMEM((1, 2 * all_tokens), F32),
            pltpu.VMEM((n_fsdp, 1, 2 * all_tokens), F32),
            pltpu.VMEM((width, 128), F32),
            pltpu.VMEM((slots, all_tokens), BF16),
            dma((n_fsdp,)), dma((n_fsdp,)),
            dma((W_CHUNKS,)), dma((W_CHUNKS,)),
            dma((14,)), dma((n_fsdp, 2)),
            dma((n_fsdp,)), dma((n_fsdp,)),
            dma((n_rep // 2,)), dma((n_rep // 2,)),
            dma((n_rep // 2,)), dma((n_rep // 2,)),
            dma((n_fsdp,)), dma((n_fsdp,)),
            dma((3,)), dma((rows // 512,)), dma((1,)), dma((1,)),
        ],
        compiler_params=pltpu.CompilerParams(
            collective_id=level, has_side_effects=True, vmem_limit_bytes=44 * 1024 * 1024
        ),
        cost_estimate=pl.CostEstimate(
            flops=6 * rows * width * all_tokens, bytes_accessed=8 * rows * width, transcendentals=all_tokens
        ),
    )


def local(weights, head_out, token_ids, embed_table, norm_gain, cotangent, mix_step):
    n_rep, n_fsdp = lax.axis_size("rep"), lax.axis_size("fsdp")
    branches = [
        make_branch(level, n_rep, n_fsdp, weights[0], head_out[0], embed_table) for level in range(MIXBITS)
    ]
    out = lax.switch(
        mix_step[0] % MIXBITS,
        branches,
        token_ids, weights[0], head_out[0], cotangent[0], embed_table, norm_gain[None],
    )
    return out[None]


def solution(mesh):
    return jax.shard_map(
        local,
        mesh=mesh,
        in_specs=(
            P("rep", None, "fsdp"),
            P("rep", "fsdp", None),
            P("rep", "fsdp"),
            P("rep", "fsdp"),
            P(),
            P("rep", "fsdp", None),
            P(),
        ),
        out_specs=P("rep", None, "fsdp"),
        check_vma=False,
    )
```

```python
import functools

import jax
import jax.numpy as jnp
from jax import lax
from jax.experimental import pallas as pl
from jax.experimental.pallas import tpu as pltpu
from jax.sharding import PartitionSpec as P

MIXBITS = 4
EPS = 1e-05
RATE = 0.5
PLACES = 8
CAP = 32
MESH = pl.DeviceIdType.MESH
F32 = jnp.float32
BF16 = jnp.bfloat16
W_CHUNKS = 8
W_SENT = ((2, 6), (3, 3), (3, 3), (3, 3))

NT = (((1,), (1,)), ((), ()))
NN = (((1,), (0,)), ((), ()))


def dot(a, b, dims):
    return lax.dot_general(a, b, dims, preferred_element_type=F32)


def kernel(
    level, n_rep, n_fsdp,
    ids_ref, w_ref, h_ref, c_ref, tab_ref, gain_ref, out_ref,
    ids_all, w_own, w_other, heads, heads_t, cot, weighted_t, table, req_out, req_in, picked, fetched, mixed_t,
    stream_t, grad_t, stat_out, stat_in, gain_col, place_of,
    ids_send, ids_recv, w_send, w_recv, h_send, h_recv, c_send, c_recv, req_send, req_recv, row_send, row_recv,
    stat_send, stat_recv, local_sem, out_sem, table_send, table_recv,
):
    tokens, heads_width = h_ref.shape
    width = w_ref.shape[1]
    rows = w_ref.shape[0]
    features = width * n_fsdp
    all_tokens = tokens * n_fsdp
    vocab = tab_ref.shape[0]
    half = tokens // 2
    chunk = rows // W_CHUNKS
    rep = lax.axis_index("rep")
    me = lax.axis_index("fsdp")
    ring = n_fsdp // 2
    place, core = me // 2, me % 2
    up = (place + 1) % ring * 2 + core
    down = (place + ring - 1) % ring * 2 + core
    across = (place + 2) % ring * 2 + core
    sibling = place * 2 + 1 - core
    side = rep // PLACES % 2
    across_z = rep + PLACES * (1 - 2 * side)
    n_peers = n_rep // 2
    my = rep // (2 * PLACES) * PLACES + rep % PLACES

    def replica(index):
        return index // PLACES * (2 * PLACES) + side * PLACES + index % PLACES

    stride = 1 << level
    w_first, w_next = W_SENT[level]
    partner = rep + stride * (1 - 2 * (rep // stride % 2))

    def remote(src, dst, send, recv, r, f):
        return pltpu.make_async_remote_copy(
            src_ref=src, dst_ref=dst, send_sem=send, recv_sem=recv, device_id=(r, f), device_id_type=MESH
        )

    own_rows = pl.ds(pl.multiple_of(me * tokens, tokens), tokens)
    local = [
        pltpu.make_async_copy(w_ref, w_own, local_sem.at[0]),
        pltpu.make_async_copy(h_ref, heads.at[own_rows], local_sem.at[1]),
        pltpu.make_async_copy(
            c_ref.at[:, pl.ds(pl.multiple_of(me * width, width), width)], cot.at[me], local_sem.at[2]
        ),
    ]
    for copy in local:
        copy.start()

    barrier = pltpu.get_barrier_semaphore()

    @pl.loop(1, n_fsdp)
    def _(step):
        pl.semaphore_signal(barrier, inc=1, device_id=(rep, (me + step) % n_fsdp), device_id_type=MESH)

    @pl.loop(1, n_peers)
    def _(step):
        pl.semaphore_signal(barrier, inc=1, device_id=(replica((my + step) % n_peers), me), device_id_type=MESH)

    pl.semaphore_signal(barrier, inc=1, device_id=(across_z, me), device_id_type=MESH)

    ids_all[me] = ids_ref[...]
    table[side] = jnp.zeros(table.shape[1:], BF16)
    table[side, :vocab] = tab_ref[...]

    pl.semaphore_wait(barrier, n_fsdp - 1 + n_peers)

    def ids_copy(step):
        peer = (me + step) % n_fsdp
        return remote(ids_all.at[me], ids_all.at[me], ids_send.at[step], ids_recv.at[me], rep, peer)

    @pl.loop(1, n_fsdp)
    def _(step):
        ids_copy(step).start()

    table_copy = remote(table.at[side], table.at[side], table_send.at[0], table_recv.at[0], across_z, me)
    table_copy.start()

    def w_copy(k):
        part = pl.ds(k * chunk, chunk)
        return remote(w_ref.at[part], w_other.at[part], w_send.at[k], w_recv.at[k], partner, me)

    for k in range(w_first):
        w_copy(k).start()

    def part_rows(owner, which):
        return pl.ds(pl.multiple_of(owner * tokens + which * half, half), half)

    def h_copy(index, owner, which, target, own=False):
        src = h_ref.at[pl.ds(which * half, half)] if own else heads.at[part_rows(owner, which)]
        return remote(
            src, heads.at[part_rows(owner, which)], h_send.at[index], h_recv.at[owner, which], rep, target
        )

    def h_wait(owner, which):
        h_copy(0, owner, which, sibling).wait_recv()

    own_sends = [
        h_copy(0, me, 0, up, True),
        h_copy(1, me, 1, down, True),
        h_copy(2, me, 1, up, True),
        h_copy(3, me, 0, down, True),
        h_copy(4, me, 0, sibling, True),
        h_copy(5, me, 1, sibling, True),
    ]
    for copy in own_sends[:2]:
        copy.start()

    def c_copy(step):
        peer = (me + step) % n_fsdp
        return remote(
            c_ref.at[:, pl.ds(pl.multiple_of(peer * width, width), width)],
            cot.at[me], c_send.at[step], c_recv.at[me], rep, peer,
        )

    gain = gain_ref[:, pl.ds(pl.multiple_of(me * width, width), width)]
    gain_col[...] = jnp.broadcast_to(gain, (128, width)).T
    earlier = jnp.where(
        lax.broadcasted_iota(jnp.int32, (tokens, tokens), 0) < lax.broadcasted_iota(jnp.int32, (tokens, tokens), 1),
        1.0,
        0.0,
    ).astype(BF16)

    def start_c():
        @pl.loop(1, n_fsdp)
        def _(step):
            c_copy(step).start()

    ring_sends = []

    def pass_on(*copies):
        for copy in copies:
            copy.start()
            ring_sends.append(copy)

    def forward():
        h_wait(down, 0)
        pass_on(h_copy(6, down, 0, up), h_copy(7, down, 0, sibling))
        h_wait(up, 1)
        pass_on(h_copy(8, up, 1, down), h_copy(9, up, 1, sibling))

    @pl.loop(1, n_fsdp)
    def _(step):
        sender = (me + step) % n_fsdp
        remote(ids_all.at[me], ids_all.at[sender], ids_send.at[step], ids_recv.at[sender], rep, sender).wait_recv()

    ids_row = jnp.concatenate([ids_all[j] for j in range(n_fsdp)], axis=1)
    owner_row = ids_row // vocab
    local_row = ids_row - owner_row * vocab + 1
    block_iota = lax.broadcasted_iota(jnp.int32, (n_rep, all_tokens), 0)
    owned = block_iota == owner_row
    owned_b = jnp.where(owned, 1.0, 0.0).astype(BF16)
    ranks = []
    seen = jnp.zeros((n_rep, 1), F32)
    for j in range(n_fsdp):
        part = slice(j * tokens, (j + 1) * tokens)
        before = dot(owned_b[:, part], earlier, NN) + seen
        ranks.append(jnp.sum(jnp.where(owned[:, part], before, 0.0), axis=0, keepdims=True))
        seen = seen + jnp.sum(jnp.where(owned[:, part], 1.0, 0.0), axis=1, keepdims=True)
    rank = jnp.concatenate(ranks, axis=1).astype(jnp.int32)
    owner_side = owner_row // PLACES % 2
    owner_peer = owner_row // (2 * PLACES) * PLACES + owner_row % PLACES
    position = (owner_peer * 2 + owner_side) * CAP + rank
    asked = lax.broadcasted_iota(jnp.int32, (n_peers, all_tokens), 0) == owner_peer
    asked_b = jnp.where(asked, 1.0, 0.0).astype(BF16)
    lane = (owner_side * 2 + my % 2) * CAP + rank
    here = lax.broadcasted_iota(jnp.int32, (128, all_tokens), 0) == lane
    high = jnp.where(here, (local_row // 2).astype(F32), 0.0).astype(BF16)
    low = jnp.where(here, (local_row % 2).astype(F32), 0.0).astype(BF16)
    counted = dot(asked_b, jnp.concatenate([high, low], axis=0), NT)
    requests = counted[:, :128] * 2.0 + counted[:, 128:]
    for v in range(n_peers):
        req_out[v] = requests[v : v + 1]
    req_in[my] = req_out[my]

    pair = PLACES
    pairs = n_peers // pair

    def req_copy(step):
        peer = (my // pair + step // pair) % pairs * pair + (my + step) % pair
        return remote(req_out.at[peer], req_in.at[my], req_send.at[step], req_recv.at[my], replica(peer), me)

    @pl.loop(1, n_peers)
    def _(step):
        req_copy(step).start()

    for k in range(w_first, w_first + w_next):
        w_copy(k).start()

    for copy in own_sends[2:]:
        copy.start()
    start_c()
    forward()

    def peer_slots(peer):
        return pl.ds(pl.multiple_of(peer * 2 * CAP, 2 * CAP), 2 * CAP)

    def row_copy(peer):
        return remote(
            picked.at[peer_slots(peer)], fetched.at[peer_slots(my)],
            row_send.at[peer], row_recv.at[my], replica(peer), me,
        )

    table_other = table.at[1 - side]
    remote(table_other, table_other, table_send.at[0], table_recv.at[0], across_z, me).wait_recv()

    @pl.loop(0, pairs)
    def _(turn):
        first = (my // pair + pairs - turn) % pairs * pair
        for j in range(pair):
            sender = first + (my + j) % pair

            @pl.when(sender != my)
            def _():
                remote(
                    req_out.at[sender], req_in.at[sender], req_send.at[0], req_recv.at[sender], replica(sender), me
                ).wait_recv()

        columns = []
        for g in range(pair // 2):
            wanted = req_in[first + 2 * g] + req_in[first + 2 * g + 1]
            columns.append(jnp.broadcast_to(wanted, (8, 128)).T[:, :1])
        row_iota = lax.broadcasted_iota(jnp.int32, (pair * CAP, table.shape[1]), 1).astype(F32) + 1.0
        for b in range(2):
            wanted_col = jnp.concatenate([c[b * 2 * CAP : (b + 1) * 2 * CAP] for c in columns], axis=0)
            found = dot(jnp.where(row_iota == wanted_col, 1.0, 0.0).astype(BF16), table[b], NN).astype(BF16)
            for j in range(pair):
                slots = pl.ds(pl.multiple_of((first + j) * 2 * CAP + b * CAP, CAP), CAP)
                picked[slots] = found[j * CAP : (j + 1) * CAP]
        for j in range(pair):
            peer = first + (my + j) % pair

            @pl.when(peer != my)
            def _():
                row_copy(peer).start()

    for k in range(w_first + w_next, W_CHUNKS):
        w_copy(k).start()

    fetched[peer_slots(my)] = picked[peer_slots(my)]

    tile = 256
    for copy in local:
        copy.wait()

    @pl.loop(0, n_rep * CAP // tile)
    def _(i):
        slot = lax.broadcasted_iota(jnp.int32, (tile, all_tokens), 0) + i * tile
        place_of[pl.ds(pl.multiple_of(i * tile, tile), tile)] = jnp.where(slot == position, 1.0, 0.0).astype(BF16)

    def token_rows(owner):
        return pl.ds(pl.multiple_of(owner * tokens, tokens), tokens)

    def turn_heads(owner):
        for b in range(heads_width // 256):
            heads_t[256 * b : 256 * (b + 1), token_rows(owner)] = heads[
                token_rows(owner), 256 * b : 256 * (b + 1)
            ].T

    def turn_cot(owner):
        weighted_t[:, token_rows(owner)] = cot[owner].astype(F32).T * gain_col[...]

    def embed(begin, end):
        @pl.loop(begin, end)
        def _(turn):
            first = (my // pair + turn) % pairs * pair
            for j in range(pair):
                v = first + j

                @pl.when(v != my)
                def _():
                    remote(
                        picked.at[peer_slots(v)], fetched.at[peer_slots(v)],
                        row_send.at[v], row_recv.at[v], replica(v), me,
                    ).wait_recv()

            slots = pl.ds(pl.multiple_of(first * 2 * CAP, pair * 2 * CAP), pair * 2 * CAP)
            rows_t = fetched[slots].T
            stream_t[...] += dot(rows_t, place_of[slots], NN)

    def mix(k):
        w_copy(k).wait_recv()
        part = pl.ds(k * chunk, chunk)
        mixed = (w_own[part].astype(F32) + w_other[part].astype(F32)) * 0.5
        mixed_t[:, part] = mixed.astype(BF16).T

    def project(k, count=1):
        part = slice(k * chunk, (k + count) * chunk)
        stream_t[...] += dot(mixed_t[:, part], heads_t[part], NN)

    def project_place(at):
        where = pl.ds(pl.multiple_of(at * 2 * tokens, 2 * tokens), 2 * tokens)
        stream_t[:, where] += dot(mixed_t[...], heads_t[:, where], NN)

    other_up = (place + 1) % ring * 2 + 1 - core
    other_down = (place + ring - 1) % ring * 2 + 1 - core
    other_across = (place + 2) % ring * 2 + 1 - core

    def finish_sends():
        @pl.loop(1, n_fsdp)
        def _(step):
            ids_copy(step).wait_send()
            c_copy(step).wait_send()

        table_copy.wait_send()

        @pl.loop(1, n_peers)
        def _(step):
            req_copy(step).wait_send()
            row_copy((my + step) % n_peers).wait_send()

        for k in range(W_CHUNKS):
            w_copy(k).wait_send()

    stream_t[...] = jnp.zeros_like(stream_t)
    turn_heads(me)
    turn_cot(me)
    h_wait(sibling, 0)
    h_wait(sibling, 1)
    turn_heads(sibling)
    h_wait(down, 1)
    h_wait(up, 0)
    pass_on(h_copy(10, down, 1, sibling), h_copy(11, up, 0, sibling))
    turn_heads(down)
    turn_heads(up)
    for owner in (other_down, other_up):
        h_wait(owner, 0)
        h_wait(owner, 1)
        turn_heads(owner)

    @pl.loop(1, n_fsdp)
    def _(step):
        sender = (me + step) % n_fsdp
        remote(cot.at[sender], cot.at[sender], c_send.at[step], c_recv.at[sender], rep, sender).wait_recv()
        turn_cot(sender)

    def take_across():
        for which in range(2):
            h_wait(across, which)
            pass_on(h_copy(12 + which, across, which, sibling))
        turn_heads(across)
        h_wait(other_across, 0)
        h_wait(other_across, 1)
        turn_heads(other_across)

    late = pairs - 1
    early = w_first + w_next
    if level == 0:
        for k in range(W_CHUNKS):
            mix(k)
        for step in (0, 1, ring - 1):
            project_place((place + step) % ring)
        embed(0, late)
        take_across()
        project_place((place + 2) % ring)
        finish_sends()
        embed(late, pairs)
    else:
        for k in range(early):
            mix(k)
        embed(0, late)
        take_across()
        project(0, early)
        embed(late, pairs)
        for k in range(early, W_CHUNKS - 1):
            mix(k)
            project(k)
        finish_sends()
        mix(W_CHUNKS - 1)
        project(W_CHUNKS - 1)

    stream = stream_t[...]
    stat_out[:, :all_tokens] = jnp.sum(stream * stream, axis=0, keepdims=True)
    stat_out[:, all_tokens:] = jnp.sum(stream * weighted_t[...], axis=0, keepdims=True)

    def stat_copy(step):
        peer = (me + step) % n_fsdp
        return remote(stat_out, stat_in.at[me], stat_send.at[step], stat_recv.at[me], rep, peer)

    for step in sorted(range(1, n_fsdp), key=lambda step: abs(2 * step - n_fsdp)):
        stat_copy(step).start()
    stat_in[me] = stat_out[...]
    for step in range(1, n_fsdp):
        sender = (me + step) % n_fsdp
        remote(stat_out, stat_in.at[sender], stat_send.at[step], stat_recv.at[sender], rep, sender).wait_recv()

    total = stat_in[0]
    for j in range(1, n_fsdp):
        total = total + stat_in[j]
    total = total * (1.0 / features)
    inverse = 1.0 / jnp.sqrt(total[:, :all_tokens] + EPS)
    scale = total[:, all_tokens:] * inverse * inverse * inverse
    grad_t[...] = (weighted_t[...] * inverse - stream_t[...] * scale).astype(BF16)

    @pl.loop(0, rows // (2 * tile))
    def _(i):
        where = pl.ds(pl.multiple_of(i * 2 * tile, 2 * tile), 2 * tile)
        grad = dot(heads_t[where], grad_t[...], NT)
        mixed = (w_own[where].astype(F32) + w_other[where].astype(F32)) * 0.5
        w_own[where] = (mixed - (RATE / all_tokens) * grad).astype(BF16)
        pltpu.make_async_copy(w_own.at[where], out_ref.at[where], out_sem.at[i]).start()

    for i in range(rows // (2 * tile)):
        where = pl.ds(i * 2 * tile, 2 * tile)
        pltpu.make_async_copy(w_own.at[where], out_ref.at[where], out_sem.at[i]).wait()
    for copy in own_sends + ring_sends:
        copy.wait_send()
    for step in range(1, n_fsdp):
        stat_copy(step).wait_send()


def make_branch(level, n_rep, n_fsdp, weights, head_out, embed_table):
    rows, width = weights.shape
    tokens, heads_width = head_out.shape
    all_tokens = tokens * n_fsdp
    vocab_pad = -(-embed_table.shape[0] // 256) * 256
    dma = pltpu.SemaphoreType.DMA
    vmem = pl.BlockSpec(memory_space=pltpu.VMEM)
    hbm = pl.BlockSpec(memory_space=pl.ANY)
    slots = n_rep * CAP
    return pl.pallas_call(
        functools.partial(kernel, level, n_rep, n_fsdp),
        name=f"step_level_{level}",
        out_shape=jax.ShapeDtypeStruct((rows, width), BF16),
        in_specs=[vmem, hbm, hbm, hbm, vmem, vmem],
        out_specs=hbm,
        scratch_shapes=[
            pltpu.VMEM((n_fsdp, 1, tokens), jnp.int32),
            pltpu.VMEM((rows, width), BF16),
            pltpu.VMEM((rows, width), BF16),
            pltpu.VMEM((all_tokens, heads_width), BF16),
            pltpu.VMEM((heads_width, all_tokens), BF16),
            pltpu.VMEM((n_fsdp, tokens, width), BF16),
            pltpu.VMEM((width, all_tokens), F32),
            pltpu.VMEM((2, vocab_pad, width), BF16),
            pltpu.VMEM((n_rep // 2, 1, 128), F32),
            pltpu.VMEM((n_rep // 2, 1, 128), F32),
            pltpu.VMEM((slots, width), BF16),
            pltpu.VMEM((slots, width), BF16),
            pltpu.VMEM((width, rows), BF16),
            pltpu.VMEM((width, all_tokens), F32),
            pltpu.VMEM((width, all_tokens), BF16),
            pltpu.VMEM((1, 2 * all_tokens), F32),
            pltpu.VMEM((n_fsdp, 1, 2 * all_tokens), F32),
            pltpu.VMEM((width, 128), F32),
            pltpu.VMEM((slots, all_tokens), BF16),
            dma((n_fsdp,)), dma((n_fsdp,)),
            dma((W_CHUNKS,)), dma((W_CHUNKS,)),
            dma((14,)), dma((n_fsdp, 2)),
            dma((n_fsdp,)), dma((n_fsdp,)),
            dma((n_rep // 2,)), dma((n_rep // 2,)),
            dma((n_rep // 2,)), dma((n_rep // 2,)),
            dma((n_fsdp,)), dma((n_fsdp,)),
            dma((3,)), dma((rows // 512,)), dma((1,)), dma((1,)),
        ],
        compiler_params=pltpu.CompilerParams(
            collective_id=level, has_side_effects=True, vmem_limit_bytes=44 * 1024 * 1024
        ),
        cost_estimate=pl.CostEstimate(
            flops=6 * rows * width * all_tokens, bytes_accessed=8 * rows * width, transcendentals=all_tokens
        ),
    )


def local(weights, head_out, token_ids, embed_table, norm_gain, cotangent, mix_step):
    n_rep, n_fsdp = lax.axis_size("rep"), lax.axis_size("fsdp")
    branches = [
        make_branch(level, n_rep, n_fsdp, weights[0], head_out[0], embed_table) for level in range(MIXBITS)
    ]
    out = lax.switch(
        mix_step[0] % MIXBITS,
        branches,
        token_ids, weights[0], head_out[0], cotangent[0], embed_table, norm_gain[None],
    )
    return out[None]


def solution(mesh):
    return jax.shard_map(
        local,
        mesh=mesh,
        in_specs=(
            P("rep", None, "fsdp"),
            P("rep", "fsdp", None),
            P("rep", "fsdp"),
            P("rep", "fsdp"),
            P(),
            P("rep", "fsdp", None),
            P(),
        ),
        out_specs=P("rep", None, "fsdp"),
        check_vma=False,
    )
```
